512 devices in a mesh: island: 16 (over y_hi, x), mp: 32 (over y_lo, z, core).
Axes of the slice: x: 4, y: 8 (y_hi: 4, y_lo: 2; y = y_hi * 2 + y_lo), z: 8, core: 2. Of those that a mesh axis runs over, the one named last changes fastest.
Arguments:
- global_params: bfloat16 [512, 12288], P(None, 'mp'), may hold values from -4 to 4
- local_params: bfloat16 [8192, 12288], P('island', 'mp'), may hold values from -16 to 16
- residual: bfloat16 [8192, 12288], P('island', 'mp'), may hold values from -4 to 4
- momentum: float32 [512, 12288], P('island', 'mp'), may hold values from -3 to 3
- kept: int32 [16, 16], replicated, may hold values from 1 to 4, as said below
- owner: int32 [64], replicated, may hold values from 0 to 15, as said below
- queries: bfloat16 [16384, 12288], P('island', 'mp'), may hold values from -6 to 6
- keys: bfloat16 [16384, 12288], P('island', 'mp'), may hold values from -6 to 6
- values: bfloat16 [16384, 12288], P('island', 'mp'), may hold values from -6 to 6
Outputs:
- merged: bfloat16 [512, 12288], P(None, 'mp')
- new_residual: bfloat16 [8192, 12288], P('island', 'mp')
- new_momentum: float32 [512, 12288], P('island', 'mp')
- attended: bfloat16 [16384, 12288], P('island', 'mp')
The draws below stay inside these ranges and needn't reach their ends.
Inputs may be any that keep to these rules, and one draw needn't show every extreme that they name: Island i sends the first kept[i, o] (in block order) of the blocks owned by island o; some owner receives 4 blocks from every island. `owner`: every island owns exactly 4 row blocks.
All inputs are finite; a program needn't handle non-finite values.
Results may differ from the reference program's by a relative error of at most 0.015.
Values may be sent and summed in bfloat16 or wider, within the bound.
No kernel may reach another device: no remote copies, remote signals or barrier semaphores. Data moves between devices by JAX's collectives and lax.ppermute only.
A program may use at most 64 MiB of HBM per device.

```python
import math
import jax
import jax.numpy as jnp
from jax import lax

D = 12288
HEAD = 128
SEQ = 1024
BLK = 8
OWN_BLK = 4
BLOCKS = 64
ROWS = 512
ALL_ROWS = 8192
TOKENS = 16384
N_ISLAND = 16


def draw_queries(key, part):
    key = jax.random.fold_in(key, 3)
    return jax.random.truncated_normal(key, -4.0, 4.0, (TOKENS, D), jnp.float32).astype(jnp.bfloat16)


def draw_keys(key, part):
    key = jax.random.fold_in(key, 4)
    return jax.random.truncated_normal(key, -4.0, 4.0, (TOKENS, D), jnp.float32).astype(jnp.bfloat16)


def draw_local_params(key, part):
    key = jax.random.fold_in(key, 5)
    column = jnp.arange(D, dtype=jnp.float32) / (D - 1)
    return (jax.random.truncated_normal(key, -3.0, 3.0, (ALL_ROWS, D), jnp.float32) * (3.0 ** column)[None, :]).astype(jnp.bfloat16)


def draw_kept(key, part):
    key = jax.random.fold_in(key, 7)
    first, second, third = jax.random.split(key, 3)
    groups = TOKENS // SEQ
    base = jax.random.randint(first, (groups, groups), 1, OWN_BLK + 1)
    full_column = jax.random.randint(second, (), 0, groups)
    low_row = jax.random.randint(third, (), 0, groups)
    columns = jnp.arange(groups)[None, :]
    rows = jnp.arange(groups)[:, None]
    base = jnp.where(columns == full_column, OWN_BLK, base)
    base = jnp.where((rows == low_row) & (columns == (full_column + 1) % groups), 1, base)
    return base.astype(jnp.int32)


def draw_owner(key, part):
    key = jax.random.fold_in(key, 9)
    order = jax.random.permutation(key, BLOCKS)
    return (order // OWN_BLK).astype(jnp.int32)


def block_scale(key, dims, cuts, smallest, largest):
    def one(position, parts):
        heights = jax.random.uniform(jax.random.fold_in(jax.random.fold_in(key, 6), position), (parts,), jnp.float32, smallest / len(cuts), largest / len(cuts))
        return jnp.repeat(jnp.exp(heights), dims[position] // parts).reshape((-1,) + (1,) * (len(dims) - position - 1))

    gain = one(*cuts[0])
    for cut in cuts[1:]:
        gain = gain * one(*cut)
    return gain


def bell_draw(own_key, dims, scale, limit, shards=(), kind=jnp.bfloat16):
    gain = block_scale(own_key, dims, shards, -0.22, 0.18) if shards else 1.0
    entries = jax.random.normal(own_key, dims, jnp.float32) * scale * gain
    return jnp.minimum(jnp.maximum(entries, -limit), limit).astype(kind)


def setup_inputs(seed: int = 0) -> dict:
    seeds = jax.random.split(jax.random.key(seed), 10)
    return {
        "global_params": bell_draw(seeds[0], (ROWS, D), 0.3, 4.0, ((1, 32),)),
        "local_params": draw_local_params(jax.random.fold_in(seeds[9], 71), 0),
        "residual": bell_draw(seeds[2], (ALL_ROWS, D), 0.5, 4.0, ((0, 16), (1, 32))),
        "momentum": bell_draw(seeds[3], (ROWS, D), 0.3, 3.0, ((0, 16), (1, 32)), jnp.float32),
        "kept": draw_kept(jax.random.fold_in(seeds[9], 71), 0),
        "owner": draw_owner(jax.random.fold_in(seeds[9], 71), 0),
        "queries": draw_queries(jax.random.fold_in(seeds[9], 71), 0),
        "keys": draw_keys(jax.random.fold_in(seeds[9], 71), 0),
        "values": bell_draw(seeds[8], (TOKENS, D), 1.0, 6.0, ((0, 16), (1, 32))),
    }


clip_level = 1.4
momentum_rate = 0.9
outer_rate = 0.7
epsilon = 1e-06

def head_attention(operands):
    query_head, key_head, value_head = operands
    scores = jnp.dot(query_head, key_head.T, preferred_element_type=jnp.float32) * (1.0 / math.sqrt(HEAD))
    positions = jnp.arange(SEQ, dtype=jnp.int32)
    causal = positions[:, None] >= positions[None, :]
    scores = jnp.where(causal, scores, -jnp.inf)
    top = lax.optimization_barrier(jnp.max(scores, axis=-1, keepdims=True))
    expo = jnp.exp(scores - top)
    probs = (expo / lax.optimization_barrier(jnp.sum(expo, axis=-1, keepdims=True))).astype(jnp.bfloat16)
    return jnp.dot(probs, value_head, preferred_element_type=jnp.float32).astype(jnp.bfloat16)

def island_attention(operands):
    query_rows, key_rows, value_rows = operands
    heads = D // HEAD
    split = lambda arr: arr.reshape(SEQ, heads, HEAD).transpose(1, 0, 2)
    result = lax.map(head_attention, (split(query_rows), split(key_rows), split(value_rows)))
    return result.transpose(1, 0, 2).reshape(SEQ, D)

def reference(global_params, local_params, residual, momentum, kept, owner, queries, keys, values):
    f32 = jnp.float32
    islands = N_ISLAND
    combined = global_params.astype(f32)[None] - local_params.reshape(islands, ROWS, D).astype(f32) + residual.reshape(islands, ROWS, D).astype(f32)
    index = jnp.arange(BLOCKS, dtype=jnp.int32)
    same = owner[None, :] == owner[:, None]
    slot_of = lax.optimization_barrier(jnp.sum((same & (index[None, :] < index[:, None])).astype(jnp.int32), axis=1))
    sent_mask = slot_of[None, :] < kept[:, owner]
    row_mask = jnp.repeat(sent_mask, BLK, axis=1)[:, :, None]
    sent = jnp.where(row_mask, combined.astype(jnp.bfloat16), jnp.zeros((), jnp.bfloat16))
    new_residual = jnp.where(row_mask, combined - sent.astype(f32), combined).astype(jnp.bfloat16)
    average = lax.optimization_barrier(jnp.sum(sent.astype(f32), axis=0)) / islands
    blockwise = average.reshape(BLOCKS, BLK, D)
    mean_square = lax.optimization_barrier(jnp.sum(blockwise * blockwise, axis=(1, 2))) / (BLK * D)
    factor = jnp.minimum(1.0, clip_level / math.sqrt(islands) / jnp.sqrt(mean_square + epsilon))
    clipped = blockwise * factor[:, None, None]
    packed_pos = owner * OWN_BLK + slot_of
    previous = momentum.reshape(BLOCKS, BLK, D)[packed_pos]
    new_moment = momentum_rate * previous + clipped
    update = clipped + momentum_rate * new_moment
    merged = (global_params.astype(f32).reshape(BLOCKS, BLK, D) - outer_rate * update).astype(jnp.bfloat16)
    moment_out = jnp.zeros((BLOCKS, BLK, D), f32).at[packed_pos].set(new_moment)
    split = lambda arr: arr.reshape(islands, SEQ, D)
    attended = lax.map(island_attention, (split(queries), split(keys), split(values)))
    return (merged.reshape(ROWS, D), new_residual.reshape(ALL_ROWS, D), moment_out.reshape(ROWS, D), attended.reshape(TOKENS, D))
```

```python
import functools
import math

import jax
import jax.numpy as jnp
from jax import lax
from jax.experimental import pallas as pl
from jax.experimental.pallas import tpu as pltpu
from jax.sharding import PartitionSpec as P

D = 12288
HEAD = 128

clip_level = 1.4
momentum_rate = 0.9
outer_rate = 0.7
epsilon = 1e-06

f32 = jnp.float32
bf16 = jnp.bfloat16
i32 = jnp.int32


def iota(shape, axis):
    return lax.broadcasted_iota(i32, shape, axis)


def places(owner_row, own_blocks):
    blocks = owner_row.shape[1]
    sub, lane = iota((blocks, blocks), 0), iota((blocks, blocks), 1)
    owner_col = jnp.sum(jnp.where(sub == lane, owner_row, 0), axis=1, keepdims=True)
    before = (owner_col == owner_row) & (lane < sub)
    slot_col = jnp.sum(before.astype(i32), axis=1, keepdims=True)
    return owner_col, slot_col, owner_col * own_blocks + slot_col


def sent_blocks(owner_col, slot_col, kept, me):
    islands = kept.shape[0]
    mine = jnp.sum(jnp.where(iota(kept.shape, 0) == me, kept, 0), axis=0, keepdims=True)
    shape = (owner_col.shape[0], islands)
    limit = jnp.sum(jnp.where(iota(shape, 1) == owner_col, mine, 0), axis=1, keepdims=True)
    return slot_col < limit


def spread_lanes(col, rows, block_rows):
    shape = (col.shape[0], rows)
    return jnp.sum(
        jnp.where(iota(shape, 1) // block_rows == iota(shape, 0), col, 0), axis=0, keepdims=True
    )


def spread_rows(col, rows, block_rows):
    blocks = col.shape[0]
    square = (blocks, blocks)
    row = jnp.sum(jnp.where(iota(square, 0) == iota(square, 1), col, 0), axis=0, keepdims=True)
    shape = (rows, blocks)
    return jnp.sum(
        jnp.where(iota(shape, 0) // block_rows == iota(shape, 1), row, 0), axis=1, keepdims=True
    )


def pack_kernel(block_rows, own_blocks, me_ref, owner_ref, kept_ref, global_ref, local_ref, residual_ref, out_ref):
    rows = global_ref.shape[0]
    owner_col, slot_col, packed_col = places(owner_ref[...], own_blocks)
    sent = sent_blocks(owner_col, slot_col, kept_ref[...], me_ref[0])
    goal = spread_lanes(jnp.where(sent, packed_col * block_rows, -rows), rows, block_rows)
    goal = goal + iota((1, rows), 1) % block_rows
    table = jnp.where(iota((rows, rows), 0) == goal, 1.0, 0.0).astype(bf16)
    combined = global_ref[...].astype(f32) - local_ref[...].astype(f32) + residual_ref[...].astype(f32)
    out_ref[...] = jnp.dot(table, combined.astype(bf16), preferred_element_type=f32).astype(bf16)


def side_kernel(block_rows, own_blocks, me_ref, owner_ref, kept_ref, global_ref, local_ref, residual_ref, new_ref, table_ref, mine_ref):
    rows = global_ref.shape[0]
    me = me_ref[0]
    owner_col, slot_col, packed_col = places(owner_ref[...], own_blocks)
    sent = sent_blocks(owner_col, slot_col, kept_ref[...], me)
    mask = spread_rows(sent.astype(i32), rows, block_rows) > 0
    fragment = global_ref[...]
    combined = fragment.astype(f32) - local_ref[...].astype(f32) + residual_ref[...].astype(f32)
    kept_part = jnp.where(mask, combined.astype(bf16).astype(f32), 0.0)
    new_ref[...] = (combined - kept_part).astype(bf16)
    goal = spread_rows(packed_col * block_rows, rows, block_rows)
    goal = goal + iota((rows, 1), 0) % block_rows
    table_ref[...] = jnp.where(iota((rows, rows), 1) == goal, 1.0, 0.0).astype(bf16)
    own_rows = own_blocks * block_rows
    place = spread_lanes(packed_col * block_rows, rows, block_rows) + iota((1, rows), 1) % block_rows
    pick = jnp.where(iota((own_rows, rows), 0) + me * own_rows == place, 1.0, 0.0).astype(bf16)
    mine_ref[...] = jnp.dot(pick, fragment, preferred_element_type=f32).astype(bf16)


def average_kernel(block_rows, received_ref, average_ref, square_ref):
    islands, own_rows, _ = received_ref.shape
    average = jnp.sum(received_ref[...].astype(f32), axis=0) / islands
    average_ref[...] = average
    squares = average * average
    lane = iota((1, 128), 1)
    row = jnp.zeros((1, 128), f32)
    for block in range(own_rows // block_rows):
        part = squares[block * block_rows : (block + 1) * block_rows]
        total = jnp.sum(jnp.sum(part, axis=0, keepdims=True), axis=1, keepdims=True)
        row = jnp.where(lane == block, total, row)
    square_ref[...] = jnp.broadcast_to(row, square_ref.shape)


def update_kernel(block_rows, islands, square_ref, average_ref, momentum_ref, mine_ref, moment_ref, fresh_ref):
    own_rows = average_ref.shape[0]
    total = jnp.sum(square_ref[...], axis=0, keepdims=True)
    root = jnp.sqrt(total / (block_rows * D) + epsilon)
    factor = jnp.minimum(1.0, clip_level / math.sqrt(islands) / root)
    lane = iota((1, 128), 1)
    for block in range(own_rows // block_rows):
        part = pl.ds(block * block_rows, block_rows)
        scale = jnp.sum(jnp.where(lane == block, factor, 0.0), axis=1, keepdims=True)
        clipped = average_ref[part, :] * scale
        moment_ref[part, :] = momentum_rate * momentum_ref[part, :] + clipped
    scales = jnp.concatenate(
        [
            jnp.broadcast_to(
                jnp.sum(jnp.where(lane == block, factor, 0.0), axis=1, keepdims=True), (block_rows, 1)
            )
            for block in range(own_rows // block_rows)
        ],
        axis=0,
    )
    update = average_ref[...] * scales + momentum_rate * moment_ref[...]
    fresh = (mine_ref[...].astype(f32) - outer_rate * update).astype(bf16)
    for island in range(islands):
        fresh_ref[island] = fresh


def merge_kernel(table_ref, fresh_ref, out_ref):
    islands, own_rows, columns = fresh_ref.shape
    fresh = fresh_ref[...].reshape(islands * own_rows, columns)
    out_ref[...] = jnp.dot(table_ref[...], fresh, preferred_element_type=f32).astype(bf16)


def attend_kernel(step, query_ref, key_ref, value_ref, out_ref):
    rows = query_ref.shape[0]
    rate = math.log2(math.e) / math.sqrt(HEAD)
    values = jnp.concatenate([value_ref[...], jnp.ones((rows, HEAD), bf16)], axis=1)
    lower = iota((step, step), 0) >= iota((step, step), 1)
    for begin in range(0, rows, step):
        end = begin + step
        query = query_ref[begin:end, :]
        across = (((1,), (1,)), ((), ()))
        corner = lax.dot_general(query, key_ref[begin:end, :], across, preferred_element_type=f32)
        corner = jnp.where(lower, corner, -jnp.inf)
        top = jnp.max(corner, axis=1, keepdims=True)
        if begin:
            past = lax.dot_general(query, key_ref[:begin, :], across, preferred_element_type=f32)
            top = jnp.maximum(top, jnp.max(past, axis=1, keepdims=True))
        expo = jnp.exp2((corner - top) * rate).astype(bf16)
        mixed = jnp.dot(expo, values[begin:end], preferred_element_type=f32)
        if begin:
            expo = jnp.exp2((past - top) * rate).astype(bf16)
            mixed = mixed + jnp.dot(expo, values[:begin], preferred_element_type=f32)
        out_ref[begin:end, :] = (mixed[:, :HEAD] / mixed[:, HEAD : HEAD + 1]).astype(bf16)


def attend(queries, keys, values):
    rows, columns = queries.shape
    heads = columns // HEAD
    head = pl.BlockSpec((rows, HEAD), lambda h: (0, h))
    return pl.pallas_call(
        functools.partial(attend_kernel, 256),
        grid=(heads,),
        in_specs=[head] * 3,
        out_specs=head,
        out_shape=jax.ShapeDtypeStruct(queries.shape, bf16),
        compiler_params=pltpu.CompilerParams(vmem_limit_bytes=32 << 20),
        cost_estimate=pl.CostEstimate(
            flops=3 * rows * rows * columns,
            bytes_accessed=8 * rows * columns,
            transcendentals=rows * rows * heads // 2,
        ),
        name="attend",
    )(queries, keys, values)


def call(body, out_shape, name, smem=0, flops=0):
    vmem = pl.BlockSpec(memory_space=pltpu.VMEM)

    def run(*args):
        return pl.pallas_call(
            body,
            in_specs=[pl.BlockSpec(memory_space=pltpu.SMEM)] * smem + [vmem] * (len(args) - smem),
            out_specs=jax.tree.map(lambda _: vmem, out_shape),
            out_shape=out_shape,
            compiler_params=pltpu.CompilerParams(vmem_limit_bytes=32 << 20),
            cost_estimate=pl.CostEstimate(flops=flops, bytes_accessed=1 << 20, transcendentals=0),
            name=name,
        )(*args)

    return run


def local(global_params, local_params, residual, momentum, kept, owner, queries, keys, values):
    islands = lax.axis_size("island")
    shards = lax.axis_size("mp")
    me = lax.axis_index("island").astype(i32).reshape(1)
    rows, columns = global_params.shape
    blocks = owner.shape[0]
    block_rows = rows // blocks
    own_blocks = blocks // islands
    own_rows = own_blocks * block_rows
    owner_row = owner.reshape(1, blocks)
    shape = jax.ShapeDtypeStruct
    outgoing = call(
        functools.partial(pack_kernel, block_rows, own_blocks),
        shape((rows, columns), bf16),
        "pack",
        smem=1,
    )(me, owner_row, kept, global_params, local_params, residual)
    received = lax.all_to_all(
        outgoing.reshape(islands, own_rows, columns), "island", split_axis=0, concat_axis=0, tiled=True
    )
    new_residual, table, mine = call(
        functools.partial(side_kernel, block_rows, own_blocks),
        (
            shape((rows, columns), bf16),
            shape((rows, rows), bf16),
            shape((own_rows, columns), bf16),
        ),
        "side",
        smem=1,
    )(me, owner_row, kept, global_params, local_params, residual)
    attended = attend(queries, keys, values)
    average, squares = call(
        functools.partial(average_kernel, block_rows),
        (shape((own_rows, columns), f32), shape((shards, 128), f32)),
        "average",
    )(received)
    squares = lax.all_to_all(squares, "mp", split_axis=0, concat_axis=0, tiled=True)
    new_moment, fresh = call(
        functools.partial(update_kernel, block_rows, islands),
        (shape((own_rows, columns), f32), shape((islands, own_rows, columns), bf16)),
        "update",
    )(squares, average, momentum, mine)
    everything = lax.all_to_all(fresh, "island", split_axis=0, concat_axis=0, tiled=True)
    merged = call(merge_kernel, shape((rows, columns), bf16), "merge")(table, everything)
    return (merged, new_residual, new_moment, attended)


def solution(mesh):
    placed = (
        P(None, "mp"),
        P("island", "mp"),
        P("island", "mp"),
        P("island", "mp"),
        P(),
        P(),
        P("island", "mp"),
        P("island", "mp"),
        P("island", "mp"),
    )
    return jax.shard_map(
        local,
        mesh=mesh,
        in_specs=placed,
        out_specs=(P(None, "mp"), P("island", "mp"), P("island", "mp"), P("island", "mp")),
        check_vma=False,
    )
```

```python
import functools
import math

import jax
import jax.numpy as jnp
from jax import lax
from jax.experimental import pallas as pl
from jax.experimental.pallas import tpu as pltpu
from jax.sharding import PartitionSpec as P

D = 12288
HEAD = 128

clip_level = 1.4
momentum_rate = 0.9
outer_rate = 0.7
epsilon = 1e-06

f32 = jnp.float32
bf16 = jnp.bfloat16
i32 = jnp.int32


def iota(shape, axis):
    return lax.broadcasted_iota(i32, shape, axis)


def places(owner_row, kept, me, rows, block_rows, own_blocks):
    blocks = owner_row.shape[1]
    islands = kept.shape[0]
    square = (blocks, blocks)
    sub, lane = iota(square, 0), iota(square, 1)
    owner_col = jnp.sum(jnp.where(sub == lane, owner_row, 0), axis=1, keepdims=True)
    before = (owner_col == owner_row) & (lane < sub)
    slot_col = jnp.sum(before.astype(i32), axis=1, keepdims=True)
    mine = jnp.sum(jnp.where(iota(kept.shape, 0) == me, kept, 0), axis=0, keepdims=True)
    hit = iota((blocks, islands), 1) == owner_col
    limit_col = jnp.sum(jnp.where(hit, mine, 0), axis=1, keepdims=True)
    place_col = (owner_col * own_blocks + slot_col) * block_rows
    wide = (blocks, rows)
    member = iota(wide, 1) // block_rows == iota(wide, 0)
    code_col = jnp.where(slot_col < limit_col, place_col, place_col + rows)
    code = jnp.sum(jnp.where(member, code_col, 0), axis=0, keepdims=True)
    return code + iota((1, rows), 1) % block_rows


def fetch(sources, targets, semaphores):
    copies = []
    for index, (source, target) in enumerate(zip(sources, targets, strict=True)):
        copies.append(pltpu.make_async_copy(source, target, semaphores.at[index]))
        copies[-1].start()
    return copies


def pieces(ref, count):
    step = ref.shape[0] // count
    return [ref.at[pl.ds(part * step, step)] for part in range(count)]


def pack_kernel(
    block_rows, own_blocks, me_ref, owner_hbm, kept_hbm, global_hbm, local_hbm, residual_hbm, out_ref,
    owner_ref, kept_ref, global_ref, local_ref, residual_ref, sem,
):
    rows = global_ref.shape[0]
    copies = fetch(
        (owner_hbm, kept_hbm, global_hbm, local_hbm, residual_hbm),
        (owner_ref, kept_ref, global_ref, local_ref, residual_ref),
        sem,
    )
    for copy in copies[:2]:
        copy.wait()
    code = places(owner_ref[...], kept_ref[...], me_ref[0], rows, block_rows, own_blocks)
    table = jnp.where(iota((rows, rows), 0) == code, 1.0, 0.0).astype(bf16)
    for copy in copies[2:]:
        copy.wait()
    combined = global_ref[...].astype(f32) - local_ref[...].astype(f32) + residual_ref[...].astype(f32)
    out_ref[...] = jnp.dot(table, combined.astype(bf16), preferred_element_type=f32).astype(bf16)


def inner_kernel(
    block_rows, own_blocks, step, me_ref, owner_hbm, kept_hbm, global_hbm, local_hbm, residual_hbm, query_ref, key_ref,
    value_ref, new_hbm, attended_hbm, table_ref, mine_ref, owner_ref, kept_ref, global_ref, local_ref, residual_ref,
    new_ref, attended_ref, in_sem, out_sem,
):
    rows = global_ref.shape[0]
    me = me_ref[0]
    copies = fetch(
        (owner_hbm, kept_hbm, global_hbm, local_hbm, residual_hbm),
        (owner_ref, kept_ref, global_ref, local_ref, residual_ref),
        in_sem,
    )
    tokens, columns = query_ref.shape
    lower = iota((step, step), 0) >= iota((step, step), 1)
    ones = jnp.ones((tokens, HEAD), bf16)
    begins = list(reversed(range(0, tokens, step)))
    stores = []

    def attend_rows(number):
        begin = begins[number]
        for head in range(columns // HEAD):
            attend_block(query_ref, key_ref, value_ref, attended_ref, lower, ones, begin, step, head)
        rng = pl.ds(begin, step)
        stores.extend(fetch((attended_ref.at[rng],), (attended_hbm.at[rng],), out_sem.at[pl.ds(number, 1)]))

    attend_rows(0)
    for copy in copies:
        copy.wait()
    code = places(owner_ref[...], kept_ref[...], me, rows, block_rows, own_blocks)
    code_col = jnp.broadcast_to(code, (8, rows)).astype(f32).T[:, :1].astype(i32)
    fragment = global_ref[...]
    combined = fragment.astype(f32) - local_ref[...].astype(f32) + residual_ref[...].astype(f32)
    kept_part = jnp.where(code_col < rows, combined.astype(bf16).astype(f32), 0.0)
    new_ref[...] = (combined - kept_part).astype(bf16)
    stores.extend(fetch((new_ref,), (new_hbm,), out_sem.at[pl.ds(len(begins), 1)]))
    place_col = jnp.where(code_col < rows, code_col, code_col - rows)
    table_ref[...] = jnp.where(iota((rows, rows), 1) == place_col, 1.0, 0.0).astype(bf16)
    own_rows = own_blocks * block_rows
    place = jnp.where(code < rows, code, code - rows)
    pick = jnp.where(iota((own_rows, rows), 0) + me * own_rows == place, 1.0, 0.0).astype(bf16)
    mine_ref[...] = jnp.dot(pick, fragment, preferred_element_type=f32).astype(bf16)
    for number in range(1, len(begins)):
        attend_rows(number)
    for copy in stores:
        copy.wait()


def attend_block(query_ref, key_ref, value_ref, out_ref, lower, ones, begin, step, head):
    rate = math.log2(math.e) / math.sqrt(HEAD)
    across = (((1,), (1,)), ((), ()))
    cols = slice(head * HEAD, (head + 1) * HEAD)
    end = begin + step
    query = query_ref[begin:end, cols]
    corner = lax.dot_general(query, key_ref[begin:end, cols], across, preferred_element_type=f32)
    corner = jnp.where(lower, corner, -jnp.inf)
    top = jnp.max(corner, axis=1, keepdims=True)
    if begin:
        past = lax.dot_general(query, key_ref[:begin, cols], across, preferred_element_type=f32)
        top = jnp.maximum(top, jnp.max(past, axis=1, keepdims=True))
    expo = jnp.exp2((corner - top) * rate).astype(bf16)
    mixed = jnp.dot(expo, jnp.concatenate([value_ref[begin:end, cols], ones[begin:end]], axis=1), preferred_element_type=f32)
    if begin:
        expo = jnp.exp2((past - top) * rate).astype(bf16)
        mixed = mixed + jnp.dot(
            expo, jnp.concatenate([value_ref[:begin, cols], ones[:begin]], axis=1), preferred_element_type=f32
        )
    out_ref[begin:end, cols] = (mixed[:, :HEAD] / mixed[:, HEAD : HEAD + 1]).astype(bf16)


def average_kernel(block_rows, received_ref, average_ref, square_ref):
    islands, own_rows, _ = received_ref.shape
    average = jnp.sum(received_ref[...].astype(f32), axis=0) / islands
    average_ref[...] = average
    squares = average * average
    lane = iota((1, 128), 1)
    row = jnp.zeros((1, 128), f32)
    for block in range(own_rows // block_rows):
        part = squares[block * block_rows : (block + 1) * block_rows]
        total = jnp.sum(jnp.sum(part, axis=0, keepdims=True), axis=1, keepdims=True)
        row = jnp.where(lane == block, total, row)
    square_ref[...] = jnp.broadcast_to(row, square_ref.shape)


def block_factors(square_ref, block_rows, own_rows, islands):
    total = jnp.sum(square_ref[...], axis=0, keepdims=True)
    root = jnp.sqrt(total / (block_rows * D) + epsilon)
    factor = jnp.minimum(1.0, clip_level / math.sqrt(islands) / root)
    shape = (own_rows, factor.shape[1])
    hit = iota(shape, 0) // block_rows == iota(shape, 1)
    return jnp.sum(jnp.where(hit, factor, 0.0), axis=1, keepdims=True)


def update_kernel(block_rows, square_ref, average_ref, momentum_ref, mine_ref, fresh_ref):
    islands, own_rows, _ = fresh_ref.shape
    clipped = average_ref[...] * block_factors(square_ref, block_rows, own_rows, islands)
    moment = momentum_rate * momentum_ref[...] + clipped
    update = clipped + momentum_rate * moment
    fresh = (mine_ref[...].astype(f32) - outer_rate * update).astype(bf16)
    for island in range(islands):
        fresh_ref[island] = fresh


def merge_kernel(
    block_rows, parts, square_ref, average_ref, momentum_ref, table_ref, fresh_ref, moment_hbm, out_hbm,
    moment_ref, out_ref, out_sem,
):
    islands, own_rows, columns = fresh_ref.shape
    clipped = average_ref[...] * block_factors(square_ref, block_rows, own_rows, islands)
    moment_ref[...] = momentum_rate * momentum_ref[...] + clipped
    stores = fetch((moment_ref,), (moment_hbm,), out_sem.at[pl.ds(parts, 1)])
    step = islands * own_rows // parts
    fresh = fresh_ref[...].reshape(islands * own_rows, columns)
    for part in range(parts):
        rng = slice(part * step, (part + 1) * step)
        out_ref[rng, :] = jnp.dot(table_ref[rng, :], fresh, preferred_element_type=f32).astype(bf16)
        rng = pl.ds(part * step, step)
        stores += fetch((out_ref.at[rng],), (out_hbm.at[rng],), out_sem.at[pl.ds(part, 1)])
    for copy in stores:
        copy.wait()


def call(body, name, in_spaces, out_spaces, out_shape, scratch=(), flops=0):
    def run(*args):
        args = [
            pltpu.with_memory_space_constraint(arg, space) if space == pltpu.HBM else arg
            for arg, space in zip(args, in_spaces, strict=True)
        ]
        return pl.pallas_call(
            body,
            in_specs=[pl.BlockSpec(memory_space=space) for space in in_spaces],
            out_specs=jax.tree.map(lambda space: pl.BlockSpec(memory_space=space), out_spaces),
            out_shape=out_shape,
            scratch_shapes=scratch,
            compiler_params=pltpu.CompilerParams(vmem_limit_bytes=32 << 20),
            cost_estimate=pl.CostEstimate(flops=flops, bytes_accessed=1 << 20, transcendentals=0),
            name=name,
        )(*args)

    return run


def local(global_params, local_params, residual, momentum, kept, owner, queries, keys, values):
    islands = lax.axis_size("island")
    shards = lax.axis_size("mp")
    me = lax.axis_index("island").astype(i32).reshape(1)
    rows, columns = global_params.shape
    tokens = queries.shape[0]
    blocks = owner.shape[0]
    block_rows = rows // blocks
    own_blocks = blocks // islands
    own_rows = own_blocks * block_rows
    owner_row = owner.reshape(1, blocks)
    shape = jax.ShapeDtypeStruct
    dma = pltpu.SemaphoreType.DMA
    vmem, smem, hbm = pltpu.VMEM, pltpu.SMEM, pltpu.HBM
    staged = [
        vmem((1, blocks), i32),
        vmem((islands, islands), i32),
        vmem((rows, columns), bf16),
        vmem((rows, columns), bf16),
        vmem((rows, columns), bf16),
    ]
    outgoing = call(
        functools.partial(pack_kernel, block_rows, own_blocks),
        "pack",
        [smem] + [hbm] * 5,
        vmem,
        shape((rows, columns), bf16),
        staged + [dma((5,))],
    )(me, owner_row, kept, global_params, local_params, residual)
    received = lax.all_to_all(
        outgoing.reshape(islands, own_rows, columns), "island", split_axis=0, concat_axis=0, tiled=True
    )
    average, squares = call(
        functools.partial(average_kernel, block_rows),
        "average",
        [vmem],
        (vmem, vmem),
        (shape((own_rows, columns), f32), shape((shards, 128), f32)),
    )(received)
    me, squares = lax.optimization_barrier((me, squares))
    squares = lax.all_to_all(squares, "mp", split_axis=0, concat_axis=0, tiled=True)
    step = min(256, tokens)
    new_residual, attended, table, mine = call(
        functools.partial(inner_kernel, block_rows, own_blocks, step),
        "inner",
        [smem] + [hbm] * 5 + [vmem] * 3,
        (hbm, hbm, vmem, vmem),
        (
            shape((rows, columns), bf16),
            shape((tokens, columns), bf16),
            shape((rows, rows), bf16),
            shape((own_rows, columns), bf16),
        ),
        staged + [vmem((rows, columns), bf16), vmem((tokens, columns), bf16), dma((5,)), dma((1 + tokens // step,))],
        flops=3 * tokens * tokens * columns,
    )(me, owner_row, kept, global_params, local_params, residual, queries, keys, values)
    fresh = call(
        functools.partial(update_kernel, block_rows),
        "update",
        [vmem] * 4,
        vmem,
        shape((islands, own_rows, columns), bf16),
    )(squares, average, momentum, mine)
    everything = lax.all_to_all(fresh, "island", split_axis=0, concat_axis=0, tiled=True)
    parts = 4
    new_moment, merged = call(
        functools.partial(merge_kernel, block_rows, parts),
        "merge",
        [vmem] * 5,
        (hbm, hbm),
        (shape((own_rows, columns), f32), shape((rows, columns), bf16)),
        [vmem((own_rows, columns), f32), vmem((rows, columns), bf16), dma((parts + 1,))],
    )(squares, average, momentum, table, everything)
    return (merged, new_residual, new_moment, attended)


def solution(mesh):
    placed = (
        P(None, "mp"),
        P("island", "mp"),
        P("island", "mp"),
        P("island", "mp"),
        P(),
        P(),
        P("island", "mp"),
        P("island", "mp"),
        P("island", "mp"),
    )
    return jax.shard_map(
        local,
        mesh=mesh,
        in_specs=placed,
        out_specs=(P(None, "mp"), P("island", "mp"), P("island", "mp"), P("island", "mp")),
        check_vma=False,
    )
```

```python
import functools
import math

import jax
import jax.numpy as jnp
from jax import lax
from jax.experimental import pallas as pl
from jax.experimental.pallas import tpu as pltpu
from jax.sharding import PartitionSpec as P

D = 12288
HEAD = 128

clip_level = 1.4
momentum_rate = 0.9
outer_rate = 0.7
epsilon = 1e-06

f32 = jnp.float32
bf16 = jnp.bfloat16
i32 = jnp.int32


def iota(shape, axis):
    return lax.broadcasted_iota(i32, shape, axis)


def places(owner_row, kept, me, rows, block_rows, own_blocks):
    blocks = owner_row.shape[1]
    islands = kept.shape[0]
    square = (blocks, blocks)
    sub, lane = iota(square, 0), iota(square, 1)
    owner_col = jnp.sum(jnp.where(sub == lane, owner_row, 0), axis=1, keepdims=True)
    before = (owner_col == owner_row) & (lane < sub)
    slot_col = jnp.sum(before.astype(i32), axis=1, keepdims=True)
    mine = jnp.sum(jnp.where(iota(kept.shape, 0) == me, kept, 0), axis=0, keepdims=True)
    hit = iota((blocks, islands), 1) == owner_col
    limit_col = jnp.sum(jnp.where(hit, mine, 0), axis=1, keepdims=True)
    place_col = (owner_col * own_blocks + slot_col) * block_rows
    wide = (blocks, rows)
    member = iota(wide, 1) // block_rows == iota(wide, 0)
    code_col = jnp.where(slot_col < limit_col, place_col, place_col + rows)
    code = jnp.sum(jnp.where(member, code_col, 0), axis=0, keepdims=True)
    return code + iota((1, rows), 1) % block_rows


def fetch(sources, targets, semaphores):
    copies = []
    for index, (source, target) in enumerate(zip(sources, targets, strict=True)):
        copies.append(pltpu.make_async_copy(source, target, semaphores.at[index]))
        copies[-1].start()
    return copies


def pieces(ref, count):
    step = ref.shape[0] // count
    return [ref.at[pl.ds(part * step, step)] for part in range(count)]


def pack_kernel(
    block_rows, own_blocks, me_ref, owner_hbm, kept_hbm, global_hbm, local_hbm, residual_hbm, out_ref, code_ref,
    owner_ref, kept_ref, global_ref, local_ref, residual_ref, sem,
):
    rows = global_ref.shape[0]
    copies = fetch(
        (owner_hbm, kept_hbm, global_hbm, local_hbm, residual_hbm),
        (owner_ref, kept_ref, global_ref, local_ref, residual_ref),
        sem,
    )
    for copy in copies[:2]:
        copy.wait()
    code = places(owner_ref[...], kept_ref[...], me_ref[0], rows, block_rows, own_blocks)
    code_ref[...] = jnp.broadcast_to(code, code_ref.shape)
    table = jnp.where(iota((rows, rows), 0) == code, 1.0, 0.0).astype(bf16)
    for copy in copies[2:]:
        copy.wait()
    combined = global_ref[...].astype(f32) - local_ref[...].astype(f32) + residual_ref[...].astype(f32)
    out_ref[...] = jnp.dot(table, combined.astype(bf16), preferred_element_type=f32).astype(bf16)


def as_column(code_ref):
    return code_ref[...].astype(f32).T[:, :1].astype(i32)


def inner_kernel(
    step, code_ref, global_hbm, local_hbm, residual_hbm, query_ref, key_ref, value_ref, new_hbm, attended_hbm,
    global_ref, local_ref, residual_ref, new_ref, attended_ref, in_sem, out_sem,
):
    rows = global_ref.shape[0]
    copies = fetch((global_hbm, local_hbm, residual_hbm), (global_ref, local_ref, residual_ref), in_sem)
    tokens, columns = query_ref.shape
    lower = iota((step, step), 0) >= iota((step, step), 1)
    ones = jnp.ones((tokens, HEAD), bf16)
    begins = list(reversed(range(0, tokens, step)))
    stores = []

    def attend_rows(number):
        begin = begins[number]
        for head in range(columns // HEAD):
            attend_block(query_ref, key_ref, value_ref, attended_ref, lower, ones, begin, step, head)
        rng = pl.ds(begin, step)
        stores.extend(fetch((attended_ref.at[rng],), (attended_hbm.at[rng],), out_sem.at[pl.ds(number, 1)]))

    attend_rows(0)
    for copy in copies:
        copy.wait()
    combined = global_ref[...].astype(f32) - local_ref[...].astype(f32) + residual_ref[...].astype(f32)
    kept_part = jnp.where(as_column(code_ref) < rows, combined.astype(bf16).astype(f32), 0.0)
    new_ref[...] = (combined - kept_part).astype(bf16)
    stores.extend(fetch((new_ref,), (new_hbm,), out_sem.at[pl.ds(len(begins), 1)]))
    for number in range(1, len(begins)):
        attend_rows(number)
    for copy in stores:
        copy.wait()


def attend_block(query_ref, key_ref, value_ref, out_ref, lower, ones, begin, step, head):
    rate = math.log2(math.e) / math.sqrt(HEAD)
    across = (((1,), (1,)), ((), ()))
    cols = slice(head * HEAD, (head + 1) * HEAD)
    end = begin + step
    query = query_ref[begin:end, cols]
    corner = lax.dot_general(query, key_ref[begin:end, cols], across, preferred_element_type=f32)
    corner = jnp.where(lower, corner, -jnp.inf)
    top = jnp.max(corner, axis=1, keepdims=True)
    if begin:
        past = lax.dot_general(query, key_ref[:begin, cols], across, preferred_element_type=f32)
        top = jnp.maximum(top, jnp.max(past, axis=1, keepdims=True))
    expo = jnp.exp2((corner - top) * rate).astype(bf16)
    mixed = jnp.dot(expo, jnp.concatenate([value_ref[begin:end, cols], ones[begin:end]], axis=1), preferred_element_type=f32)
    if begin:
        expo = jnp.exp2((past - top) * rate).astype(bf16)
        mixed = mixed + jnp.dot(
            expo, jnp.concatenate([value_ref[:begin, cols], ones[:begin]], axis=1), preferred_element_type=f32
        )
    out_ref[begin:end, cols] = (mixed[:, :HEAD] / mixed[:, HEAD : HEAD + 1]).astype(bf16)


def average_kernel(
    block_rows, me_ref, received_ref, code_ref, global_ref, average_ref, square_hbm, table_ref, mine_ref, square_ref, sem
):
    islands, own_rows, _ = received_ref.shape
    average = jnp.sum(received_ref[...].astype(f32), axis=0) / islands
    average_ref[...] = average
    squares = average * average
    lane = iota((1, 128), 1)
    row = jnp.zeros((1, 128), f32)
    for block in range(own_rows // block_rows):
        part = squares[block * block_rows : (block + 1) * block_rows]
        total = jnp.sum(jnp.sum(part, axis=0, keepdims=True), axis=1, keepdims=True)
        row = jnp.where(lane == block, total, row)
    square_ref[...] = jnp.broadcast_to(row, square_ref.shape)
    stores = fetch((square_ref,), (square_hbm,), sem)
    rows = global_ref.shape[0]
    code = code_ref[0:1, :]
    place = jnp.where(code < rows, code, code - rows)
    pick = jnp.where(iota((own_rows, rows), 0) + me_ref[0] * own_rows == place, 1.0, 0.0).astype(bf16)
    mine_ref[...] = jnp.dot(pick, global_ref[...], preferred_element_type=f32).astype(bf16)
    code_col = as_column(code_ref)
    place_col = jnp.where(code_col < rows, code_col, code_col - rows)
    table_ref[...] = jnp.where(iota((rows, rows), 1) == place_col, 1.0, 0.0).astype(bf16)
    for copy in stores:
        copy.wait()


def block_factors(square_ref, block_rows, own_rows, islands):
    total = jnp.sum(square_ref[...], axis=0, keepdims=True)
    root = jnp.sqrt(total / (block_rows * D) + epsilon)
    factor = jnp.minimum(1.0, clip_level / math.sqrt(islands) / root)
    shape = (own_rows, factor.shape[1])
    hit = iota(shape, 0) // block_rows == iota(shape, 1)
    return jnp.sum(jnp.where(hit, factor, 0.0), axis=1, keepdims=True)


def update_kernel(block_rows, square_ref, average_ref, momentum_ref, mine_ref, fresh_ref):
    islands, own_rows, _ = fresh_ref.shape
    clipped = average_ref[...] * block_factors(square_ref, block_rows, own_rows, islands)
    moment = momentum_rate * momentum_ref[...] + clipped
    update = clipped + momentum_rate * moment
    fresh = (mine_ref[...].astype(f32) - outer_rate * update).astype(bf16)
    for island in range(islands):
        fresh_ref[island] = fresh


def merge_kernel(
    block_rows, parts, square_ref, average_ref, momentum_ref, table_ref, fresh_ref, moment_hbm, out_hbm,
    moment_ref, out_ref, out_sem,
):
    islands, own_rows, columns = fresh_ref.shape
    clipped = average_ref[...] * block_factors(square_ref, block_rows, own_rows, islands)
    moment_ref[...] = momentum_rate * momentum_ref[...] + clipped
    stores = fetch((moment_ref,), (moment_hbm,), out_sem.at[pl.ds(parts, 1)])
    step = islands * own_rows // parts
    fresh = fresh_ref[...].reshape(islands * own_rows, columns)
    for part in range(parts):
        rng = slice(part * step, (part + 1) * step)
        out_ref[rng, :] = jnp.dot(table_ref[rng, :], fresh, preferred_element_type=f32).astype(bf16)
        rng = pl.ds(part * step, step)
        stores += fetch((out_ref.at[rng],), (out_hbm.at[rng],), out_sem.at[pl.ds(part, 1)])
    for copy in stores:
        copy.wait()


def call(body, name, in_spaces, out_spaces, out_shape, scratch=(), flops=0):
    def run(*args):
        args = [
            pltpu.with_memory_space_constraint(arg, space) if space == pltpu.HBM else arg
            for arg, space in zip(args, in_spaces, strict=True)
        ]
        return pl.pallas_call(
            body,
            in_specs=[pl.BlockSpec(memory_space=space) for space in in_spaces],
            out_specs=jax.tree.map(lambda space: pl.BlockSpec(memory_space=space), out_spaces),
            out_shape=out_shape,
            scratch_shapes=scratch,
            compiler_params=pltpu.CompilerParams(vmem_limit_bytes=32 << 20),
            cost_estimate=pl.CostEstimate(flops=flops, bytes_accessed=1 << 20, transcendentals=0),
            name=name,
        )(*args)

    return run


def local(global_params, local_params, residual, momentum, kept, owner, queries, keys, values):
    islands = lax.axis_size("island")
    shards = lax.axis_size("mp")
    me = lax.axis_index("island").astype(i32).reshape(1)
    rows, columns = global_params.shape
    tokens = queries.shape[0]
    blocks = owner.shape[0]
    block_rows = rows // blocks
    own_blocks = blocks // islands
    own_rows = own_blocks * block_rows
    owner_row = owner.reshape(1, blocks)
    shape = jax.ShapeDtypeStruct
    dma = pltpu.SemaphoreType.DMA
    vmem, smem, hbm = pltpu.VMEM, pltpu.SMEM, pltpu.HBM
    staged = [
        vmem((1, blocks), i32),
        vmem((islands, islands), i32),
        vmem((rows, columns), bf16),
        vmem((rows, columns), bf16),
        vmem((rows, columns), bf16),
    ]
    outgoing, code = call(
        functools.partial(pack_kernel, block_rows, own_blocks),
        "pack",
        [smem] + [hbm] * 5,
        (vmem, vmem),
        (shape((rows, columns), bf16), shape((8, rows), i32)),
        staged + [dma((5,))],
    )(me, owner_row, kept, global_params, local_params, residual)
    outgoing, queries, keys, values, momentum = lax.optimization_barrier(
        (outgoing, queries, keys, values, momentum)
    )
    received = lax.all_to_all(
        outgoing.reshape(islands, own_rows, columns), "island", split_axis=0, concat_axis=0, tiled=True
    )
    average, squares, table, mine = call(
        functools.partial(average_kernel, block_rows),
        "average",
        [smem] + [vmem] * 3,
        (vmem, hbm, vmem, vmem),
        (
            shape((own_rows, columns), f32),
            shape((shards, 128), f32),
            shape((rows, rows), bf16),
            shape((own_rows, columns), bf16),
        ),
        [vmem((shards, 128), f32), dma((1,))],
    )(me, received, code, global_params)
    code, squares = lax.optimization_barrier((code, squares))
    squares = lax.all_to_all(squares, "mp", split_axis=0, concat_axis=0, tiled=True)
    step = min(256, tokens)
    new_residual, attended = call(
        functools.partial(inner_kernel, step),
        "inner",
        [vmem] + [hbm] * 3 + [vmem] * 3,
        (hbm, hbm),
        (shape((rows, columns), bf16), shape((tokens, columns), bf16)),
        staged[2:]
        + [vmem((rows, columns), bf16), vmem((tokens, columns), bf16), dma((3,)), dma((1 + tokens // step,))],
        flops=3 * tokens * tokens * columns,
    )(code, global_params, local_params, residual, queries, keys, values)
    mine, new_residual = lax.optimization_barrier((mine, new_residual))
    fresh = call(
        functools.partial(update_kernel, block_rows),
        "update",
        [vmem] * 4,
        vmem,
        shape((islands, own_rows, columns), bf16),
    )(squares, average, momentum, mine)
    everything = lax.all_to_all(fresh, "island", split_axis=0, concat_axis=0, tiled=True)
    parts = 4
    new_moment, merged = call(
        functools.partial(merge_kernel, block_rows, parts),
        "merge",
        [vmem] * 5,
        (hbm, hbm),
        (shape((own_rows, columns), f32), shape((rows, columns), bf16)),
        [vmem((own_rows, columns), f32), vmem((rows, columns), bf16), dma((parts + 1,))],
    )(squares, average, momentum, table, everything)
    return (merged, new_residual, new_moment, attended)


def solution(mesh):
    placed = (
        P(None, "mp"),
        P("island", "mp"),
        P("island", "mp"),
        P("island", "mp"),
        P(),
        P(),
        P("island", "mp"),
        P("island", "mp"),
        P("island", "mp"),
    )
    return jax.shard_map(
        local,
        mesh=mesh,
        in_specs=placed,
        out_specs=(P(None, "mp"), P("island", "mp"), P("island", "mp"), P("island", "mp")),
        check_vma=False,
    )
```

```python
import functools
import math

import jax
import jax.numpy as jnp
from jax import lax
from jax.experimental import pallas as pl
from jax.experimental.pallas import tpu as pltpu
from jax.sharding import PartitionSpec as P

D = 12288
HEAD = 128

clip_level = 1.4
momentum_rate = 0.9
outer_rate = 0.7
epsilon = 1e-06

f32 = jnp.float32
bf16 = jnp.bfloat16
i32 = jnp.int32


def iota(shape, axis):
    return lax.broadcasted_iota(i32, shape, axis)


def places(owner_row, kept, me, rows, block_rows, own_blocks):
    blocks = owner_row.shape[1]
    islands = kept.shape[0]
    square = (blocks, blocks)
    sub, lane = iota(square, 0), iota(square, 1)
    owner_col = jnp.sum(jnp.where(sub == lane, owner_row, 0), axis=1, keepdims=True)
    before = (owner_col == owner_row) & (lane < sub)
    slot_col = jnp.sum(before.astype(i32), axis=1, keepdims=True)
    mine = jnp.sum(jnp.where(iota(kept.shape, 0) == me, kept, 0), axis=0, keepdims=True)
    hit = iota((blocks, islands), 1) == owner_col
    limit_col = jnp.sum(jnp.where(hit, mine, 0), axis=1, keepdims=True)
    place_col = (owner_col * own_blocks + slot_col) * block_rows
    wide = (blocks, rows)
    member = iota(wide, 1) // block_rows == iota(wide, 0)
    code_col = jnp.where(slot_col < limit_col, place_col, place_col + rows)
    code = jnp.sum(jnp.where(member, code_col, 0), axis=0, keepdims=True)
    return code + iota((1, rows), 1) % block_rows


def fetch(sources, targets, semaphores):
    copies = []
    for index, (source, target) in enumerate(zip(sources, targets, strict=True)):
        copies.append(pltpu.make_async_copy(source, target, semaphores.at[index]))
        copies[-1].start()
    return copies


def pieces(ref, count):
    step = ref.shape[0] // count
    return [ref.at[pl.ds(part * step, step)] for part in range(count)]


def pack_kernel(
    block_rows, own_blocks, me_ref, owner_hbm, kept_hbm, global_hbm, local_hbm, residual_hbm, out_ref,
    owner_ref, kept_ref, global_ref, local_ref, residual_ref, sem,
):
    rows = global_ref.shape[0]
    copies = fetch(
        (owner_hbm, kept_hbm, global_hbm, local_hbm, residual_hbm),
        (owner_ref, kept_ref, global_ref, local_ref, residual_ref),
        sem,
    )
    for copy in copies[:2]:
        copy.wait()
    code = places(owner_ref[...], kept_ref[...], me_ref[0], rows, block_rows, own_blocks)
    table = jnp.where(iota((rows, rows), 0) == code, 1.0, 0.0).astype(bf16)
    for copy in copies[2:]:
        copy.wait()
    combined = global_ref[...].astype(f32) - local_ref[...].astype(f32) + residual_ref[...].astype(f32)
    out_ref[...] = jnp.dot(table, combined.astype(bf16), preferred_element_type=f32).astype(bf16)


def inner_kernel(
    block_rows, own_blocks, step, me_ref, owner_hbm, kept_hbm, global_hbm, local_hbm, residual_hbm, query_ref, key_ref,
    value_ref, new_hbm, attended_hbm, table_ref, mine_ref, owner_ref, kept_ref, global_ref, local_ref, residual_ref,
    new_ref, attended_ref, in_sem, out_sem,
):
    rows = global_ref.shape[0]
    me = me_ref[0]
    copies = fetch(
        (owner_hbm, kept_hbm, global_hbm, local_hbm, residual_hbm),
        (owner_ref, kept_ref, global_ref, local_ref, residual_ref),
        in_sem,
    )
    tokens, columns = query_ref.shape
    lower = iota((step, step), 0) >= iota((step, step), 1)
    ones = jnp.ones((tokens, HEAD), bf16)
    begins = list(reversed(range(0, tokens, step)))
    stores = []

    def attend_rows(number):
        begin = begins[number]
        for head in range(columns // HEAD):
            attend_block(query_ref, key_ref, value_ref, attended_ref, lower, ones, begin, step, head)
        rng = pl.ds(begin, step)
        stores.extend(fetch((attended_ref.at[rng],), (attended_hbm.at[rng],), out_sem.at[pl.ds(number, 1)]))

    attend_rows(0)
    for copy in copies:
        copy.wait()
    code = places(owner_ref[...], kept_ref[...], me, rows, block_rows, own_blocks)
    code_col = jnp.broadcast_to(code, (8, rows)).astype(f32).T[:, :1].astype(i32)
    fragment = global_ref[...]
    combined = fragment.astype(f32) - local_ref[...].astype(f32) + residual_ref[...].astype(f32)
    kept_part = jnp.where(code_col < rows, combined.astype(bf16).astype(f32), 0.0)
    new_ref[...] = (combined - kept_part).astype(bf16)
    stores.extend(fetch((new_ref,), (new_hbm,), out_sem.at[pl.ds(len(begins), 1)]))
    place_col = jnp.where(code_col < rows, code_col, code_col - rows)
    table_ref[...] = jnp.where(iota((rows, rows), 1) == place_col, 1.0, 0.0).astype(bf16)
    own_rows = own_blocks * block_rows
    place = jnp.where(code < rows, code, code - rows)
    pick = jnp.where(iota((own_rows, rows), 0) + me * own_rows == place, 1.0, 0.0).astype(bf16)
    mine_ref[...] = jnp.dot(pick, fragment, preferred_element_type=f32).astype(bf16)
    for number in range(1, len(begins)):
        attend_rows(number)
    for copy in stores:
        copy.wait()


def attend_block(query_ref, key_ref, value_ref, out_ref, lower, ones, begin, step, head):
    rate = math.log2(math.e) / math.sqrt(HEAD)
    across = (((1,), (1,)), ((), ()))
    cols = slice(head * HEAD, (head + 1) * HEAD)
    end = begin + step
    query = query_ref[begin:end, cols]
    corner = lax.dot_general(query, key_ref[begin:end, cols], across, preferred_element_type=f32)
    corner = jnp.where(lower, corner, -jnp.inf)
    top = jnp.max(corner, axis=1, keepdims=True)
    if begin:
        past = lax.dot_general(query, key_ref[:begin, cols], across, preferred_element_type=f32)
        top = jnp.maximum(top, jnp.max(past, axis=1, keepdims=True))
    expo = jnp.exp2((corner - top) * rate).astype(bf16)
    mixed = jnp.dot(expo, jnp.concatenate([value_ref[begin:end, cols], ones[begin:end]], axis=1), preferred_element_type=f32)
    if begin:
        expo = jnp.exp2((past - top) * rate).astype(bf16)
        mixed = mixed + jnp.dot(
            expo, jnp.concatenate([value_ref[:begin, cols], ones[:begin]], axis=1), preferred_element_type=f32
        )
    out_ref[begin:end, cols] = (mixed[:, :HEAD] / mixed[:, HEAD : HEAD + 1]).astype(bf16)


def average_kernel(block_rows, received_ref, average_ref, square_hbm, square_ref, sem):
    islands, own_rows, _ = received_ref.shape
    lane = iota((1, 128), 1)
    row = jnp.zeros((1, 128), f32)
    for block in range(own_rows // block_rows):
        part = slice(block * block_rows, (block + 1) * block_rows)
        average = jnp.sum(received_ref[...].astype(f32)[:, part], axis=0) / islands
        average_ref[part, :] = average
        total = jnp.sum(jnp.sum(average * average, axis=0, keepdims=True), axis=1, keepdims=True)
        row = jnp.where(lane == block, total, row)
    square_ref[...] = jnp.broadcast_to(row, square_ref.shape)
    for copy in fetch((square_ref,), (square_hbm,), sem):
        copy.wait()


def block_factors(square_ref, block_rows, own_rows, islands):
    total = jnp.sum(square_ref[...], axis=0, keepdims=True)
    root = jnp.sqrt(total / (block_rows * D) + epsilon)
    factor = jnp.minimum(1.0, clip_level / math.sqrt(islands) / root)
    shape = (own_rows, factor.shape[1])
    hit = iota(shape, 0) // block_rows == iota(shape, 1)
    return jnp.sum(jnp.where(hit, factor, 0.0), axis=1, keepdims=True)


def update_kernel(block_rows, square_ref, average_ref, momentum_ref, mine_ref, fresh_ref):
    islands, own_rows, _ = fresh_ref.shape
    clipped = average_ref[...] * block_factors(square_ref, block_rows, own_rows, islands)
    moment = momentum_rate * momentum_ref[...] + clipped
    update = clipped + momentum_rate * moment
    fresh = (mine_ref[...].astype(f32) - outer_rate * update).astype(bf16)
    for island in range(islands):
        fresh_ref[island] = fresh


def merge_kernel(
    block_rows, parts, square_ref, average_ref, momentum_ref, table_ref, fresh_ref, moment_hbm, out_hbm,
    moment_ref, out_ref, out_sem,
):
    islands, own_rows, columns = fresh_ref.shape
    clipped = average_ref[...] * block_factors(square_ref, block_rows, own_rows, islands)
    moment_ref[...] = momentum_rate * momentum_ref[...] + clipped
    stores = fetch((moment_ref,), (moment_hbm,), out_sem.at[pl.ds(parts, 1)])
    step = islands * own_rows // parts
    fresh = fresh_ref[...].reshape(islands * own_rows, columns)
    for part in range(parts):
        rng = slice(part * step, (part + 1) * step)
        out_ref[rng, :] = jnp.dot(table_ref[rng, :], fresh, preferred_element_type=f32).astype(bf16)
        rng = pl.ds(part * step, step)
        stores += fetch((out_ref.at[rng],), (out_hbm.at[rng],), out_sem.at[pl.ds(part, 1)])
    for copy in stores:
        copy.wait()


def call(body, name, in_spaces, out_spaces, out_shape, scratch=(), flops=0):
    def run(*args):
        args = [
            pltpu.with_memory_space_constraint(arg, space) if space == pltpu.HBM else arg
            for arg, space in zip(args, in_spaces, strict=True)
        ]
        return pl.pallas_call(
            body,
            in_specs=[pl.BlockSpec(memory_space=space) for space in in_spaces],
            out_specs=jax.tree.map(lambda space: pl.BlockSpec(memory_space=space), out_spaces),
            out_shape=out_shape,
            scratch_shapes=scratch,
            compiler_params=pltpu.CompilerParams(vmem_limit_bytes=32 << 20),
            cost_estimate=pl.CostEstimate(flops=flops, bytes_accessed=1 << 20, transcendentals=0),
            name=name,
        )(*args)

    return run


def local(global_params, local_params, residual, momentum, kept, owner, queries, keys, values):
    islands = lax.axis_size("island")
    shards = lax.axis_size("mp")
    me = lax.axis_index("island").astype(i32).reshape(1)
    rows, columns = global_params.shape
    tokens = queries.shape[0]
    blocks = owner.shape[0]
    block_rows = rows // blocks
    own_blocks = blocks // islands
    own_rows = own_blocks * block_rows
    owner_row = owner.reshape(1, blocks)
    shape = jax.ShapeDtypeStruct
    dma = pltpu.SemaphoreType.DMA
    vmem, smem, hbm = pltpu.VMEM, pltpu.SMEM, pltpu.HBM
    staged = [
        vmem((1, blocks), i32),
        vmem((islands, islands), i32),
        vmem((rows, columns), bf16),
        vmem((rows, columns), bf16),
        vmem((rows, columns), bf16),
    ]
    outgoing = call(
        functools.partial(pack_kernel, block_rows, own_blocks),
        "pack",
        [smem] + [hbm] * 5,
        vmem,
        shape((rows, columns), bf16),
        staged + [dma((5,))],
    )(me, owner_row, kept, global_params, local_params, residual)
    outgoing, queries, keys, values, momentum = lax.optimization_barrier((outgoing, queries, keys, values, momentum))
    received = lax.all_to_all(
        outgoing.reshape(islands, own_rows, columns), "island", split_axis=0, concat_axis=0, tiled=True
    )
    average, squares = call(
        functools.partial(average_kernel, block_rows),
        "average",
        [vmem],
        (vmem, hbm),
        (shape((own_rows, columns), f32), shape((shards, 128), f32)),
        [vmem((shards, 128), f32), dma((1,))],
    )(received)
    me, squares = lax.optimization_barrier((me, squares))
    squares = lax.all_to_all(squares, "mp", split_axis=0, concat_axis=0, tiled=True)
    step = min(256, tokens)
    new_residual, attended, table, mine = call(
        functools.partial(inner_kernel, block_rows, own_blocks, step),
        "inner",
        [smem] + [hbm] * 5 + [vmem] * 3,
        (hbm, hbm, vmem, vmem),
        (
            shape((rows, columns), bf16),
            shape((tokens, columns), bf16),
            shape((rows, rows), bf16),
            shape((own_rows, columns), bf16),
        ),
        staged + [vmem((rows, columns), bf16), vmem((tokens, columns), bf16), dma((5,)), dma((1 + tokens // step,))],
        flops=3 * tokens * tokens * columns,
    )(me, owner_row, kept, global_params, local_params, residual, queries, keys, values)
    fresh = call(
        functools.partial(update_kernel, block_rows),
        "update",
        [vmem] * 4,
        vmem,
        shape((islands, own_rows, columns), bf16),
    )(squares, average, momentum, mine)
    everything = lax.all_to_all(fresh, "island", split_axis=0, concat_axis=0, tiled=True)
    parts = 4
    new_moment, merged = call(
        functools.partial(merge_kernel, block_rows, parts),
        "merge",
        [vmem] * 5,
        (hbm, hbm),
        (shape((own_rows, columns), f32), shape((rows, columns), bf16)),
        [vmem((own_rows, columns), f32), vmem((rows, columns), bf16), dma((parts + 1,))],
    )(squares, average, momentum, table, everything)
    return (merged, new_residual, new_moment, attended)


def solution(mesh):
    placed = (
        P(None, "mp"),
        P("island", "mp"),
        P("island", "mp"),
        P("island", "mp"),
        P(),
        P(),
        P("island", "mp"),
        P("island", "mp"),
        P("island", "mp"),
    )
    return jax.shard_map(
        local,
        mesh=mesh,
        in_specs=placed,
        out_specs=(P(None, "mp"), P("island", "mp"), P("island", "mp"), P("island", "mp")),
        check_vma=False,
    )
```
